32 devices in a mesh: parts: 2 (over x), row: 16 (over z, y, core).
Axes of the slice: x: 2, y: 2, z: 4, core: 2. Of those that a mesh axis runs over, the one named last changes fastest.
Arguments:
- train_grads: bfloat16 [32768, 4096], P(('parts', 'row')), parts along dimension 0, may hold values from -140 to 140
- query_grads: bfloat16 [256, 4096], P(('parts', 'row')), parts along dimension 0, may hold values from -140 to 140
- inverse_gram: bfloat16 [4096, 4096], P('row'), may hold values from -0.5 to 3.5, as said below
Outputs:
- scores: bfloat16 [32768, 128], P(('parts', 'row')), parts along dimension 0
The draws below stay inside these ranges and needn't reach their ends.
There are 2 independent parts, one for each index of `parts`. The reference program is written for one: setup_inputs(seed, part) draws one part's arguments, and reference() takes and returns one part's arrays. A program takes and returns all parts, laid end to end along the dimension named above; an argument that names none is the same for every part. Nothing has to cross between parts.
Inputs may be any that keep to these rules, and one draw needn't show every extreme that they name: `inverse_gram`: symmetric.
All inputs are finite; a program needn't handle non-finite values.
Results may differ from the reference program's by a relative error of at most 0.0051.
Values may be sent and summed in bfloat16 or wider, within the bound.
A program may use at most 64 MiB of HBM per device.

```python
import math
import jax
import jax.numpy as jnp
from jax import lax

PROJ = 4096
N_TRAIN = 16384
N_QUERY = 128


def scaled_rows(key, base, rows, top):
    first, second = jax.random.split(key)
    row_part = jnp.exp(jax.random.uniform(first, (rows, 1), jnp.float32) * math.log(top))
    col_part = jnp.exp(jax.random.uniform(second, (1, PROJ), jnp.float32, -0.7, 0.7))
    return base * row_part * col_part


def draw_train_grads(key, part):
    key = jax.random.fold_in(key, 11)
    first, second = jax.random.split(key)
    base = jnp.clip(jax.random.normal(first, (N_TRAIN, PROJ), jnp.float32), -4.0, 4.0)
    values = scaled_rows(second, base, N_TRAIN, 10.0)
    return values.astype(jnp.bfloat16)


def draw_query_grads(key, part):
    key = jax.random.fold_in(key, 23)
    first, second = jax.random.split(key)
    base = jnp.clip(jax.random.normal(first, (N_QUERY, PROJ), jnp.float32), -4.0, 4.0)
    values = scaled_rows(second, base, N_QUERY, 10.0)
    return values.astype(jnp.bfloat16)


def draw_inverse_gram(key, part):
    key = jax.random.fold_in(key, 37)
    first, second = jax.random.split(key)
    loose = jnp.clip(jax.random.normal(first, (PROJ, PROJ), jnp.float32), -4.0, 4.0)
    diag_part = jax.random.uniform(second, (PROJ, 1), jnp.float32, 1.0, 2.0)
    sym = (loose + loose.T) * (0.6 / math.sqrt(PROJ))
    return (sym + jnp.eye(PROJ, dtype=jnp.float32) * diag_part).astype(jnp.bfloat16)


def setup_inputs(seed: int = 0, part: int = 0) -> dict:
    arg_keys = jax.random.split(jax.random.key(seed), 4)
    own_keys = jax.random.split(jax.random.fold_in(arg_keys[3], part), 4)
    return {
        "train_grads": draw_train_grads(jax.random.fold_in(jax.random.fold_in(arg_keys[3], part), 71), part),
        "query_grads": draw_query_grads(jax.random.fold_in(jax.random.fold_in(arg_keys[3], part), 71), part),
        "inverse_gram": draw_inverse_gram(jax.random.fold_in(arg_keys[3], 71), part),
    }


def inverse_rms(values):
    wide = values.astype(jnp.float32)
    return lax.rsqrt(lax.optimization_barrier(jnp.mean(wide * wide, axis=1)) + 1e-06)

def reference(train_grads, query_grads, inverse_gram):
    precond = jnp.dot(query_grads, inverse_gram, preferred_element_type=jnp.float32).astype(jnp.bfloat16)
    train_scale = inverse_rms(train_grads)
    query_scale = inverse_rms(precond)
    raw = lax.dot_general(train_grads, precond, (((1,), (1,)), ((), ())), preferred_element_type=jnp.float32)
    factor = 1.0 / PROJ ** 0.5
    return (raw * train_scale[:, None] * query_scale[None, :] * factor).astype(jnp.bfloat16)
```

```python
import functools

import jax
import jax.numpy as jnp
from jax import lax
from jax.experimental import pallas as pl
from jax.experimental.pallas import tpu as pltpu
from jax.sharding import PartitionSpec as P

CORES = 2
LANES = 128
T_CHUNKS = 8


def flip(value, bits):
    out = value
    bit = 1
    while bit <= bits:
        if bits & bit:
            out = out + bit - 2 * bit * ((out // bit) % 2)
        bit *= 2
    return out


class Gather:
    def __init__(self, dims, slots, recv, send_z, send_y, send_c):
        self.dims = dims
        self.slots, self.recv = slots, recv
        self.send_z, self.send_y, self.send_c = send_z, send_y, send_c
        me = lax.axis_index("row")
        depth, width = dims
        self.c = me % CORES
        self.y = (me // CORES) % width
        self.z = me // (CORES * width)
        self.sends = []

    def row(self, z, y, c):
        return (z * self.dims[1] + y) * CORES + c

    def block(self, dz, dy, dc):
        return self.row(flip(self.z, dz), flip(self.y, dy), flip(self.c, dc))

    def push(self, j, to, sem):
        copy = pltpu.make_async_remote_copy(
            src_ref=self.slots.at[j],
            dst_ref=self.slots.at[j],
            send_sem=sem,
            recv_sem=self.recv.at[j],
            device_id={"row": to},
            device_id_type=pl.DeviceIdType.MESH,
        )
        copy.start()
        self.sends.append(copy)

    def pass_on(self, dz, dy):
        depth, width = self.dims
        j = self.block(dz, dy, 0)
        if dy == 0:
            for k in range(1, width):
                self.push(j, self.block(0, k, 0), self.send_y.at[dz * (width - 1) + k - 1])
        self.push(j, self.block(0, 0, 1), self.send_c.at[dz * width + dy])

    def begin(self):
        depth, width = self.dims
        j = self.block(0, 0, 0)
        for dz in reversed(range(1, depth)):
            self.push(j, self.block(dz, 0, 0), self.send_z.at[dz - 1])
        self.pass_on(0, 0)

    def arrive(self, dz, dy, dc):
        j = self.block(dz, dy, dc)
        slot = self.slots.at[j]
        pltpu.make_async_remote_copy(
            src_ref=slot, dst_ref=slot, send_sem=self.recv.at[j], recv_sem=self.recv.at[j],
            device_id={"row": self.block(0, 0, 1)}, device_id_type=pl.DeviceIdType.MESH,
        ).wait_recv()
        if dc == 0:
            self.pass_on(dz, dy)

    def order(self):
        depth, width = self.dims
        steps = []
        for dz in range(depth):
            if dz:
                steps.append((dz, 0, 0))
            steps.append((dz, 0, 1))
            for dy in range(1, width):
                if dz == 0:
                    continue
                steps.append((dz - 1, dy, 0))
                steps.append((dz - 1, dy, 1))
        for dy in range(1, width):
            steps.append((depth - 1, dy, 0))
            steps.append((depth - 1, dy, 1))
        return steps

    def finish(self):
        for copy in self.sends:
            copy.wait_send()


def kernel(dims, t_hbm, q_ref, g_hbm, out_ref, t_ref, g_ref, q_all, p_all, acc, scale, ssq, t_sem, g_sem,
           q_recv, q_z, q_y, q_c, p_recv, p_z, p_y, p_c):
    depth, width = dims
    n = depth * width * CORES
    rows, proj = t_ref.shape
    blk = g_ref.shape[0]
    nq = out_ref.shape[1]
    tile = rows // T_CHUNKS

    g_copy = pltpu.make_async_copy(g_hbm, g_ref, g_sem)
    g_copy.start()
    t_copies = []
    for i in range(T_CHUNKS):
        span = pl.ds(i * tile, tile)
        t_copies.append(pltpu.make_async_copy(t_hbm.at[span], t_ref.at[span], t_sem.at[i]))
        t_copies[-1].start()

    q_gather = Gather(dims, q_all, q_recv, q_z, q_y, q_c)
    p_gather = Gather(dims, p_all, p_recv, p_z, p_y, p_c)
    me = q_gather.block(0, 0, 0)

    barrier = pltpu.get_barrier_semaphore()
    peers = [q_gather.block(dz, 0, 0) for dz in range(1, depth)]
    peers += [q_gather.block(0, dy, 0) for dy in range(1, width)]
    peers += [q_gather.block(0, 0, 1)]
    for peer in peers:
        pl.semaphore_signal(barrier, inc=1, device_id={"row": peer}, device_id_type=pl.DeviceIdType.MESH)
    q_all[me] = q_ref[...]
    pl.semaphore_wait(barrier, len(peers))

    q_gather.begin()

    def row_scale(i):
        t_copies[i].wait()

        @pl.loop(0, tile // 16)
        def _(s):
            span = pl.ds(pl.multiple_of(i * tile + s * 16, 16), 16)
            total = jnp.zeros((16, LANES), jnp.float32)
            for k in range(proj // LANES):
                wide = t_ref[span, k * LANES:(k + 1) * LANES].astype(jnp.float32)
                total += wide * wide
            mean = jnp.sum(total, axis=1, keepdims=True) * (1.0 / proj)
            scale[span, :] = jnp.broadcast_to(lax.rsqrt(mean + 1e-06), (16, LANES))

    todo = list(range(T_CHUNKS))
    for step in q_gather.order():
        if todo:
            row_scale(todo.pop(0))
        q_gather.arrive(*step)
    for i in todo:
        row_scale(i)
    g_copy.wait()

    queries = q_all[...].astype(jnp.float32).reshape(nq, proj).astype(jnp.bfloat16)
    mine = lax.dot_general(
        g_ref[...], queries, (((1,), (1,)), ((), ())), preferred_element_type=jnp.float32
    ).astype(jnp.bfloat16)
    p_all[me] = mine
    p_gather.begin()

    def add_ssq(j, first=False):
        wide = p_all[j].astype(jnp.float32)
        part = jnp.sum(wide * wide, axis=0, keepdims=True)
        ssq[...] = part if first else ssq[...] + part

    aligned = blk % LANES == 0

    def add(j, first=False):
        add_ssq(j, first)
        if not aligned:
            return
        columns = pl.ds(pl.multiple_of(j * blk, blk), blk)
        part = jnp.dot(t_ref[:, columns], p_all[j], preferred_element_type=jnp.float32)
        acc[...] = part if first else acc[...] + part

    add(me, True)
    for step in p_gather.order():
        p_gather.arrive(*step)
        add(p_gather.block(*step))
    if not aligned:
        panel = p_all[...].reshape(proj, nq)
        acc[...] = jnp.dot(t_ref[...], panel, preferred_element_type=jnp.float32)

    query_scale = lax.rsqrt(ssq[...] * (1.0 / proj) + 1e-06)
    factor = 1.0 / proj ** 0.5
    for k in range(nq // LANES):
        span = slice(k * LANES, (k + 1) * LANES)
        out_ref[:, span] = (acc[:, span] * scale[...] * query_scale[:, span] * factor).astype(out_ref.dtype)
    q_gather.finish()
    p_gather.finish()


def solution(mesh):
    n = mesh.shape["row"]
    width = 2 if mesh.shape["parts"] == 2 else 1
    depth = n // (CORES * width)

    def body(train_grads, query_grads, inverse_gram):
        rows, proj = train_grads.shape
        own = query_grads.shape[0]
        nq = own * n
        blk = inverse_gram.shape[0]
        dma = pltpu.SemaphoreType.DMA
        sems = [
            dma((n,)),
            dma((depth - 1,)),
            dma((max(1, depth * (width - 1)),)),
            dma((depth * width,)),
        ]
        return pl.pallas_call(
            functools.partial(kernel, (depth, width)),
            out_shape=jax.ShapeDtypeStruct((rows, nq), jnp.bfloat16),
            in_specs=[
                pl.BlockSpec(memory_space=pl.ANY),
                pl.BlockSpec(memory_space=pltpu.VMEM),
                pl.BlockSpec(memory_space=pl.ANY),
            ],
            out_specs=pl.BlockSpec(memory_space=pltpu.VMEM),
            scratch_shapes=[
                pltpu.VMEM((rows, proj), jnp.bfloat16),
                pltpu.VMEM((blk, proj), jnp.bfloat16),
                pltpu.VMEM((n, own, proj), jnp.bfloat16),
                pltpu.VMEM((n, blk, nq), jnp.bfloat16),
                pltpu.VMEM((rows, nq), jnp.float32),
                pltpu.VMEM((rows, LANES), jnp.float32),
                pltpu.VMEM((1, nq), jnp.float32),
                dma((T_CHUNKS,)),
                dma,
                *sems,
                *sems,
            ],
            compiler_params=pltpu.CompilerParams(
                collective_id=0, has_side_effects=True, vmem_limit_bytes=56 * 1024 * 1024
            ),
        )(train_grads, query_grads, inverse_gram)

    return jax.shard_map(
        body,
        mesh=mesh,
        in_specs=(P(("parts", "row"), None), P(("parts", "row"), None), P("row", None)),
        out_specs=P(("parts", "row"), None),
        check_vma=False,
    )
```

```python
import functools

import jax
import jax.numpy as jnp
from jax import lax
from jax.experimental import pallas as pl
from jax.experimental.pallas import tpu as pltpu
from jax.sharding import PartitionSpec as P

CORES = 2
LANES = 128
T_CHUNKS = 8
Q_PIECES = 1
P_PIECES = 1


def flip(value, bits):
    out = value
    bit = 1
    while bit <= bits:
        if bits & bit:
            out = out + bit - 2 * bit * ((out // bit) % 2)
        bit *= 2
    return out


class Gather:
    def __init__(self, dims, slots, recv, sent):
        self.dims = dims
        self.slots, self.recv, self.sent = slots, recv, sent
        me = lax.axis_index("row")
        depth, width = dims
        self.c = me % CORES
        self.y = (me // CORES) % width
        self.z = me // (CORES * width)
        self.sends = []

    def block(self, dz, dy, dc):
        z, y, c = flip(self.z, dz), flip(self.y, dy), flip(self.c, dc)
        return (z * self.dims[1] + y) * CORES + c

    def push(self, j, piece, to):
        slot = self.slots.at[j, piece]
        copy = pltpu.make_async_remote_copy(
            src_ref=slot,
            dst_ref=slot,
            send_sem=self.sent.at[len(self.sends)],
            recv_sem=self.recv.at[j, piece],
            device_id={"row": to},
            device_id_type=pl.DeviceIdType.MESH,
        )
        copy.start()
        self.sends.append(copy)

    def step(self, entry):
        block, piece, targets = entry
        j = self.block(*block)
        if block != (0, 0, 0):
            slot = self.slots.at[j, piece]
            pltpu.make_async_remote_copy(
                src_ref=slot,
                dst_ref=slot,
                send_sem=self.recv.at[j, piece],
                recv_sem=self.recv.at[j, piece],
                device_id={"row": self.block(0, 0, 1)},
                device_id_type=pl.DeviceIdType.MESH,
            ).wait_recv()
        for target in targets:
            self.push(j, piece, self.block(*target))

    def finish(self):
        for copy in self.sends:
            copy.wait_send()


def make_plan(dims, pieces):
    depth, width = dims
    across = [(0, dy, 0) for dy in range(1, width)]
    core = [(0, 0, 1)]
    routes = {(dz, 0, 0): across + core for dz in range(1, depth)}
    routes.update({(dz, dy, 0): core for dz in range(depth) for dy in range(1, width)})
    first = [(1, 0, 0)] + across + core + [(dz, 0, 0) for dz in range(2, depth)]
    order = [(1, 0, 0)] + across
    for dz in range(2, depth):
        order += [(dz, 0, 0)] + [(dz - 1, dy, 0) for dy in range(1, width)]
    order += [(depth - 1, dy, 0) for dy in range(1, width)]
    plan = [((0, 0, 0), p, first) for p in range(pieces)]
    plan += [(block, p, routes[block]) for block in order for p in range(pieces)]
    late = [((block[0], block[1], 1), p, []) for block, p, _ in plan]
    return plan, late


def kernel(dims, t_hbm, q_ref, g_hbm, out_ref, t_ref, g_ref, q_all, p_all, acc, squares, ssq, t_sem, g_sem,
           q_recv, q_sent, p_recv, p_sent):
    depth, width = dims
    rows, proj = t_ref.shape
    blk = g_ref.shape[0]
    own, nq = q_ref.shape[0], out_ref.shape[1]
    tile = rows // T_CHUNKS

    g_copy = pltpu.make_async_copy(g_hbm, g_ref, g_sem)
    g_copy.start()
    t_copies = []
    for i in range(T_CHUNKS):
        span = pl.ds(i * tile, tile)
        t_copies.append(pltpu.make_async_copy(t_hbm.at[span], t_ref.at[span], t_sem.at[i]))
        t_copies[-1].start()

    q_gather = Gather(dims, q_all, q_recv, q_sent)
    p_gather = Gather(dims, p_all, p_recv, p_sent)
    me = q_gather.block(0, 0, 0)

    barrier = pltpu.get_barrier_semaphore()
    peers = []
    for _, _, targets in make_plan(dims, 1)[0]:
        peers += [target for target in targets if target not in peers]
    peers = [q_gather.block(*peer) for peer in peers]
    for peer in peers:
        pl.semaphore_signal(barrier, inc=1, device_id={"row": peer}, device_id_type=pl.DeviceIdType.MESH)
    cut = proj // Q_PIECES
    for p in range(Q_PIECES):
        q_all[me, p] = q_ref[:, p * cut:(p + 1) * cut]
    pl.semaphore_wait(barrier, len(peers))

    def row_squares(i):
        t_copies[i].wait()

        @pl.loop(0, tile // 32)
        def _(s):
            span = pl.ds(pl.multiple_of(i * tile + s * 32, 32), 32)
            total = jnp.zeros((32, LANES), jnp.float32)
            for k in range(proj // LANES):
                wide = t_ref[span, k * LANES:(k + 1) * LANES].astype(jnp.float32)
                total += wide * wide
            squares[span, :] = total

    todo = list(range(T_CHUNKS))
    plan, late = make_plan(dims, Q_PIECES)
    for entry in plan:
        q_gather.step(entry)
        if todo and entry[1] == Q_PIECES - 1:
            row_squares(todo.pop(0))
    for entry in late:
        q_gather.step(entry)
    for i in todo:
        row_squares(i)
    g_copy.wait()

    mine = None
    for p in range(Q_PIECES):
        queries = q_all[:, p].astype(jnp.float32).reshape(nq, cut).astype(jnp.bfloat16)
        part = lax.dot_general(
            g_ref[:, p * cut:(p + 1) * cut], queries, (((1,), (1,)), ((), ())),
            preferred_element_type=jnp.float32,
        )
        mine = part if mine is None else mine + part
    panel = mine.astype(jnp.bfloat16)
    high = blk // P_PIECES
    for p in range(P_PIECES):
        p_all[me, p] = panel[p * high:(p + 1) * high]

    aligned = blk % LANES == 0

    def add(j, first=False):
        block = p_all[j].reshape(blk, nq)
        wide = block.astype(jnp.float32)
        part = jnp.sum(wide * wide, axis=0, keepdims=True)
        ssq[...] = part if first else ssq[...] + part
        if not aligned:
            return
        columns = pl.ds(pl.multiple_of(j * blk, blk), blk)
        part = jnp.dot(t_ref[:, columns], block, preferred_element_type=jnp.float32)
        acc[...] = part if first else acc[...] + part

    plan, late = make_plan(dims, P_PIECES)
    done = []
    for entry in plan:
        p_gather.step(entry)
        if entry[1] == P_PIECES - 1:
            add(p_gather.block(*entry[0]), not done)
            done.append(entry[0])
            if len(done) > 2:
                for other in late:
                    if other[0][:2] == done[-3][:2]:
                        p_gather.step(other)
                add(p_gather.block(*done[-3][:2], 1))
    for block in done[-2:]:
        for other in late:
            if other[0][:2] == block[:2]:
                p_gather.step(other)
        add(p_gather.block(*block[:2], 1))
    if not aligned:
        whole = p_all[...].reshape(proj, nq)
        acc[...] = jnp.dot(t_ref[...], whole, preferred_element_type=jnp.float32)

    scale = lax.rsqrt(jnp.sum(squares[...], axis=1, keepdims=True) * (1.0 / proj) + 1e-06)
    query_scale = lax.rsqrt(ssq[...] * (1.0 / proj) + 1e-06)
    factor = 1.0 / proj ** 0.5
    out_ref[...] = (acc[...] * scale * query_scale * factor).astype(out_ref.dtype)
    q_gather.finish()
    p_gather.finish()


def solution(mesh):
    n = mesh.shape["row"]
    width = 2 if mesh.shape["parts"] == 2 else 1
    depth = n // (CORES * width)

    def body(train_grads, query_grads, inverse_gram):
        rows, proj = train_grads.shape
        own = query_grads.shape[0]
        nq = own * n
        blk = inverse_gram.shape[0]
        dma = pltpu.SemaphoreType.DMA

        def sems(pieces):
            plan, late = make_plan((depth, width), pieces)
            return [dma((n, pieces)), dma((sum(len(entry[2]) for entry in plan),))]

        return pl.pallas_call(
            functools.partial(kernel, (depth, width)),
            out_shape=jax.ShapeDtypeStruct((rows, nq), jnp.bfloat16),
            in_specs=[
                pl.BlockSpec(memory_space=pl.ANY),
                pl.BlockSpec(memory_space=pltpu.VMEM),
                pl.BlockSpec(memory_space=pl.ANY),
            ],
            out_specs=pl.BlockSpec(memory_space=pltpu.VMEM),
            scratch_shapes=[
                pltpu.VMEM((rows, proj), jnp.bfloat16),
                pltpu.VMEM((blk, proj), jnp.bfloat16),
                pltpu.VMEM((n, Q_PIECES, own, proj // Q_PIECES), jnp.bfloat16),
                pltpu.VMEM((n, P_PIECES, blk // P_PIECES, nq), jnp.bfloat16),
                pltpu.VMEM((rows, nq), jnp.float32),
                pltpu.VMEM((rows, LANES), jnp.float32),
                pltpu.VMEM((1, nq), jnp.float32),
                dma((T_CHUNKS,)),
                dma,
                *sems(Q_PIECES),
                *sems(P_PIECES),
            ],
            compiler_params=pltpu.CompilerParams(
                collective_id=0, has_side_effects=True, vmem_limit_bytes=56 * 1024 * 1024
            ),
        )(train_grads, query_grads, inverse_gram)

    return jax.shard_map(
        body,
        mesh=mesh,
        in_specs=(P(("parts", "row"), None), P(("parts", "row"), None), P("row", None)),
        out_specs=P(("parts", "row"), None),
        check_vma=False,
    )
```

```python
import functools

import jax
import jax.numpy as jnp
from jax import lax
from jax.experimental import pallas as pl
from jax.experimental.pallas import tpu as pltpu
from jax.sharding import PartitionSpec as P

CORES = 2
LANES = 128
T_CHUNKS = 16
Q_PIECES = 1
P_PIECES = 1


def flip(value, bits):
    out = value
    bit = 1
    while bit <= bits:
        if bits & bit:
            out = out + bit - 2 * bit * ((out // bit) % 2)
        bit *= 2
    return out


class Gather:
    def __init__(self, dims, slots, recv, sent):
        self.dims = dims
        self.slots, self.recv, self.sent = slots, recv, sent
        me = lax.axis_index("row")
        depth, width = dims
        self.c = me % CORES
        self.y = (me // CORES) % width
        self.z = me // (CORES * width)
        self.sends = []

    def block(self, dz, dy, dc):
        z, y, c = flip(self.z, dz), flip(self.y, dy), flip(self.c, dc)
        return (z * self.dims[1] + y) * CORES + c

    def push(self, j, piece, to):
        slot = self.slots.at[j, piece]
        copy = pltpu.make_async_remote_copy(
            src_ref=slot,
            dst_ref=slot,
            send_sem=self.sent.at[len(self.sends)],
            recv_sem=self.recv.at[j, piece],
            device_id={"row": to},
            device_id_type=pl.DeviceIdType.MESH,
        )
        copy.start()
        self.sends.append(copy)

    def step(self, entry):
        block, piece, targets = entry
        j = self.block(*block)
        if block != (0, 0, 0):
            slot = self.slots.at[j, piece]
            pltpu.make_async_remote_copy(
                src_ref=slot,
                dst_ref=slot,
                send_sem=self.recv.at[j, piece],
                recv_sem=self.recv.at[j, piece],
                device_id={"row": self.block(0, 0, 1)},
                device_id_type=pl.DeviceIdType.MESH,
            ).wait_recv()
        for target in targets:
            self.push(j, piece, self.block(*target))

    def finish(self):
        for copy in self.sends:
            copy.wait_send()


def make_plan(dims, pieces):
    depth, width = dims
    across = [(0, dy, 0) for dy in range(1, width)]
    core = [(0, 0, 1)]
    routes = {(dz, 0, 0): across + core for dz in range(1, depth)}
    routes.update({(dz, dy, 0): core for dz in range(depth) for dy in range(1, width)})
    first = [(1, 0, 0)] + across + core + [(dz, 0, 0) for dz in range(2, depth)]
    order = [(1, 0, 0)] + across
    for dz in range(2, depth):
        order += [(dz, 0, 0)] + [(dz - 1, dy, 0) for dy in range(1, width)]
    order += [(depth - 1, dy, 0) for dy in range(1, width)]
    plan = [((0, 0, 0), p, first) for p in range(pieces)]
    plan += [(block, p, routes[block]) for block in order for p in range(pieces)]
    late = [((block[0], block[1], 1), p, []) for block, p, _ in plan]
    return plan, late


def kernel(dims, t_hbm, q_ref, g_hbm, out_ref, t_ref, g_ref, q_all, p_all, acc, squares, ssq, t_sem, g_sem,
           q_recv, q_sent, p_recv, p_sent):
    depth, width = dims
    rows, proj = t_ref.shape
    blk = g_ref.shape[0]
    own, nq = q_ref.shape[0], out_ref.shape[1]
    tile = rows // T_CHUNKS

    g_copy = pltpu.make_async_copy(g_hbm, g_ref, g_sem)
    g_copy.start()
    t_copies = []
    for i in range(T_CHUNKS):
        span = pl.ds(i * tile, tile)
        t_copies.append(pltpu.make_async_copy(t_hbm.at[span], t_ref.at[span], t_sem.at[i]))
        t_copies[-1].start()

    q_gather = Gather(dims, q_all, q_recv, q_sent)
    p_gather = Gather(dims, p_all, p_recv, p_sent)
    me = q_gather.block(0, 0, 0)

    barrier = pltpu.get_barrier_semaphore()
    peers = []
    for _, _, targets in make_plan(dims, 1)[0]:
        peers += [target for target in targets if target not in peers]
    peers = [q_gather.block(*peer) for peer in peers]
    for peer in peers:
        pl.semaphore_signal(barrier, inc=1, device_id={"row": peer}, device_id_type=pl.DeviceIdType.MESH)
    cut = proj // Q_PIECES
    for p in range(Q_PIECES):
        q_all[me, p] = q_ref[:, p * cut:(p + 1) * cut]
    pl.semaphore_wait(barrier, len(peers))

    def row_squares(i):
        t_copies[i].wait()

        @pl.loop(0, tile // 32)
        def _(s):
            span = pl.ds(pl.multiple_of(i * tile + s * 32, 32), 32)
            total = jnp.zeros((32, LANES), jnp.float32)
            for k in range(proj // LANES):
                wide = t_ref[span, k * LANES:(k + 1) * LANES].astype(jnp.float32)
                total += wide * wide
            squares[span, :] = total

    todo = list(range(T_CHUNKS))
    plan, late = make_plan(dims, Q_PIECES)
    for entry in plan:
        q_gather.step(entry)
        if todo and entry[1] == Q_PIECES - 1:
            row_squares(todo.pop(0))
    for entry in late:
        if todo:
            row_squares(todo.pop(0))
        q_gather.step(entry)
    for i in todo:
        row_squares(i)
    g_copy.wait()

    mine = None
    for p in range(Q_PIECES):
        queries = q_all[:, p].astype(jnp.float32).reshape(nq, cut).astype(jnp.bfloat16)
        part = lax.dot_general(
            g_ref[:, p * cut:(p + 1) * cut], queries, (((1,), (1,)), ((), ())),
            preferred_element_type=jnp.float32,
        )
        mine = part if mine is None else mine + part
    panel = mine.astype(jnp.bfloat16)
    high = blk // P_PIECES
    for p in range(P_PIECES):
        p_all[me, p] = panel[p * high:(p + 1) * high]

    aligned = blk % LANES == 0

    def add(j, first=False):
        block = p_all[j].reshape(blk, nq)
        wide = block.astype(jnp.float32)
        part = jnp.sum(wide * wide, axis=0, keepdims=True)
        ssq[...] = part if first else ssq[...] + part
        if not aligned:
            return
        columns = pl.ds(pl.multiple_of(j * blk, blk), blk)
        part = jnp.dot(t_ref[:, columns], block, preferred_element_type=jnp.float32)
        acc[...] = part if first else acc[...] + part

    factor = 1.0 / proj ** 0.5

    def row_scale():
        total = jnp.sum(squares[...], axis=1, keepdims=True)
        scale = lax.rsqrt(total * (1.0 / proj) + 1e-06) * factor
        squares[...] = jnp.broadcast_to(scale, squares.shape)

    plan, late = make_plan(dims, P_PIECES)
    done = []
    for entry in plan:
        p_gather.step(entry)
        if entry[1] == P_PIECES - 1:
            add(p_gather.block(*entry[0]), not done)
            if not done:
                row_scale()
            done.append(entry[0])
            if len(done) > 2:
                for other in late:
                    if other[0][:2] == done[-3][:2]:
                        p_gather.step(other)
                add(p_gather.block(*done[-3][:2], 1))
    for block in done[-2:]:
        for other in late:
            if other[0][:2] == block[:2]:
                p_gather.step(other)
        add(p_gather.block(*block[:2], 1))
    if not aligned:
        whole = p_all[...].reshape(proj, nq)
        acc[...] = jnp.dot(t_ref[...], whole, preferred_element_type=jnp.float32)

    query_scale = lax.rsqrt(ssq[...] * (1.0 / proj) + 1e-06)
    for k in range(nq // LANES):
        span = slice(k * LANES, (k + 1) * LANES)
        out_ref[:, span] = (acc[:, span] * squares[...] * query_scale[:, span]).astype(out_ref.dtype)
    q_gather.finish()
    p_gather.finish()


def solution(mesh):
    n = mesh.shape["row"]
    width = 2 if mesh.shape["parts"] == 2 else 1
    depth = n // (CORES * width)

    def body(train_grads, query_grads, inverse_gram):
        rows, proj = train_grads.shape
        own = query_grads.shape[0]
        nq = own * n
        blk = inverse_gram.shape[0]
        dma = pltpu.SemaphoreType.DMA

        def sems(pieces):
            plan, late = make_plan((depth, width), pieces)
            return [dma((n, pieces)), dma((sum(len(entry[2]) for entry in plan),))]

        return pl.pallas_call(
            functools.partial(kernel, (depth, width)),
            out_shape=jax.ShapeDtypeStruct((rows, nq), jnp.bfloat16),
            in_specs=[
                pl.BlockSpec(memory_space=pl.ANY),
                pl.BlockSpec(memory_space=pltpu.VMEM),
                pl.BlockSpec(memory_space=pl.ANY),
            ],
            out_specs=pl.BlockSpec(memory_space=pltpu.VMEM),
            scratch_shapes=[
                pltpu.VMEM((rows, proj), jnp.bfloat16),
                pltpu.VMEM((blk, proj), jnp.bfloat16),
                pltpu.VMEM((n, Q_PIECES, own, proj // Q_PIECES), jnp.bfloat16),
                pltpu.VMEM((n, P_PIECES, blk // P_PIECES, nq), jnp.bfloat16),
                pltpu.VMEM((rows, nq), jnp.float32),
                pltpu.VMEM((rows, LANES), jnp.float32),
                pltpu.VMEM((1, nq), jnp.float32),
                dma((T_CHUNKS,)),
                dma,
                *sems(Q_PIECES),
                *sems(P_PIECES),
            ],
            compiler_params=pltpu.CompilerParams(
                collective_id=0, has_side_effects=True, vmem_limit_bytes=56 * 1024 * 1024
            ),
        )(train_grads, query_grads, inverse_gram)

    return jax.shard_map(
        body,
        mesh=mesh,
        in_specs=(P(("parts", "row"), None), P(("parts", "row"), None), P("row", None)),
        out_specs=P(("parts", "row"), None),
        check_vma=False,
    )
```
